32 devices in a mesh: aa: 4 (over y, x), ba: 4 (over z), col: 2 (over core).
Axes of the slice: x: 2, y: 2, z: 4, core: 2. Of those that a mesh axis runs over, the one named last changes fastest.
Arguments:
- tensor: bfloat16 [1024, 512, 256], P('aa', 'ba', 'col'), may hold values from -6 to 6
- factor_two: bfloat16 [512, 64], P('ba'), may hold values from -0.25 to 0.25
- factor_three: bfloat16 [256, 64], P('col'), may hold values from -0.375 to 0.375
Outputs:
- gram: float32 [1024, 1024], P('aa', ('ba', 'col'))
The draws below stay inside these ranges and needn't reach their ends.
All inputs are finite; a program needn't handle non-finite values.
Results may differ from the reference program's by a relative error of at most 0.008.
Values sent between devices are 32-bit elements; how exact they have to be, the bound alone decides.
No kernel may reach another device: no remote copies, remote signals or barrier semaphores. Data moves between devices by JAX's collectives and lax.ppermute only.
A program may use at most 64 MiB of HBM per device.

```python
import jax
import jax.numpy as jnp
from jax import lax

R = 64
C1 = 256
I1 = 1024
I2 = 512
I3 = 256


def steps_of(rng, dims, split, low, top_value):
    factor_of, own = 1.0, jax.random.fold_in(rng, 6)
    for axis_at, shards_of in split:
        heights = jnp.exp(jax.random.uniform(jax.random.fold_in(own, axis_at), (shards_of,), jnp.float32, low / len(split), top_value / len(split)))
        factor_of = factor_of * jnp.repeat(heights, dims[axis_at] // shards_of).reshape([-1 if axis == axis_at else 1 for axis in range(len(dims))])
    return factor_of


def bell_draw(stream_key, dims, spread, most, pieces=(), held_as=jnp.bfloat16):
    gain = steps_of(stream_key, dims, pieces, -0.22, 0.18) if pieces else 1.0
    entries = jax.random.normal(stream_key, dims, jnp.float32) * spread * gain
    return jnp.minimum(jnp.maximum(entries, -most), most).astype(held_as)


def setup_inputs(seed: int = 0) -> dict:
    key_list = jax.random.split(jax.random.key(seed), 4)
    tensor = bell_draw(key_list[0], (I1, I2, I3), 1.0, 6.0, ((0, 4), (1, 4), (2, 2)))
    factor_two = bell_draw(key_list[1], (I2, R), I2 ** -0.5, 0.25, ((0, 4),))
    factor_three = bell_draw(key_list[2], (I3, R), I3 ** -0.5, 0.375, ((0, 2),))
    return {"tensor": tensor, "factor_two": factor_two, "factor_three": factor_three}


def reference(tensor, factor_two, factor_three):
    second = factor_two.astype(jnp.float32)
    third = factor_three.astype(jnp.float32)
    blocks = tensor.reshape(I1 // C1, C1, I2, I3)

    def project(block):
        values = block.astype(jnp.float32)
        partial_value = jnp.einsum("ijk,ks->ijs", values, third, precision=lax.Precision.HIGHEST)
        partial_value = partial_value.astype(jnp.bfloat16).astype(jnp.float32)
        result = jnp.einsum("ijs,jr->irs", partial_value, second, precision=lax.Precision.HIGHEST)
        return result.reshape(C1, R * R)

    projected = lax.map(project, blocks).reshape(I1, R * R)
    gram = jnp.dot(projected, projected.T, precision=lax.Precision.HIGHEST, preferred_element_type=jnp.float32)
    return gram * (1.0 / (R * R))
```

```python
import functools

import jax
import jax.numpy as jnp
from jax import lax
from jax.experimental import pallas as pl
from jax.experimental.pallas import tpu as pltpu
from jax.sharding import PartitionSpec as P

UNIT = 16
HALF = UNIT // 2
CHUNKS = (3, 3, 2)


def reversed_bits(value, count):
    return sum(((value >> k) & 1) << (count - 1 - k) for k in range(count))


def bits_of(n):
    return n.bit_length() - 1


def exchange(x, axis, distance):
    n = lax.axis_size(axis)
    return lax.ppermute(x, axis, [(i, i ^ distance) for i in range(n)])


def project_kernel(place, n_col, n_mid, tensor_ref, two_ref, three_ref, out_ref, two_s, three_s):
    rank = three_ref.shape[0]
    block = rank // n_mid

    @pl.when((pl.program_id(0) == 0) & (pl.program_id(1) == 0))
    def _():
        wide = two_ref[...].astype(jnp.float32)
        out_ref[0, :, : wide.shape[1]] = wide
        rows = []
        for position in range(n_mid):
            at = place[1] ^ reversed_bits(n_mid - 1 - position, bits_of(n_mid))
            rows.append(out_ref[0, pl.ds(pl.multiple_of(at * block, block), block), : wide.shape[1]])
        two_s[...] = jnp.concatenate(rows, axis=0).astype(jnp.bfloat16)
        three = three_ref[...]
        zero = jnp.zeros_like(three)
        three_s[...] = jnp.concatenate(
            [jnp.concatenate([three, zero], axis=1), jnp.concatenate([zero, three], axis=1)], axis=0
        )

    values = tensor_ref[...]
    _, n_two, n_three = values.shape
    pairs = jnp.concatenate([values[:HALF], values[HALF:]], axis=2).reshape(HALF * n_two, 2 * n_three)
    partial_value = lax.dot_general(
        pairs, three_s[...], (((1,), (1,)), ((), ())), preferred_element_type=jnp.float32
    ).astype(jnp.bfloat16)
    partial_value = partial_value.reshape(HALF, n_two, 2 * rank)
    wide = jnp.concatenate([partial_value[p] for p in range(HALF)], axis=1)
    out_ref[0] = jnp.dot(two_s[...], wide, preferred_element_type=jnp.float32)


def project(place, tensor, two_t, three_t, first, count, n_col, n_mid, per_core):
    rows, n_two, n_three = tensor.shape
    rank = two_t.shape[0]
    width = UNIT * rank

    def block_at(position, unit, place):
        core = place[0]
        for p in range(n_col):
            flip = reversed_bits(n_col - 1 - p, bits_of(n_col))
            core = jnp.where(position == p, place[0] ^ flip, core)
        at = (first + unit) * UNIT
        h, t = at // per_core, at % per_core
        return (h * n_col * per_core + core * per_core + t) // UNIT

    return pl.pallas_call(
        lambda place, *refs: project_kernel(place, n_col, n_mid, *refs),
        out_shape=jax.ShapeDtypeStruct((n_col, rank, count * width), jnp.float32),
        grid_spec=pltpu.PrefetchScalarGridSpec(
            num_scalar_prefetch=1,
            grid=(n_col, count),
            in_specs=[
                pl.BlockSpec((UNIT, n_two, n_three), lambda p, u, place: (block_at(p, u, place), 0, 0)),
                pl.BlockSpec((rank, n_two), lambda p, u, place: (0, 0)),
                pl.BlockSpec((rank, n_three), lambda p, u, place: (0, 0)),
            ],
            out_specs=pl.BlockSpec((1, rank, width), lambda p, u, place: (p, 0, u)),
            scratch_shapes=[
                pltpu.VMEM((rank, n_two), jnp.bfloat16),
                pltpu.VMEM((2 * rank, 2 * n_three), jnp.bfloat16),
            ],
        ),
        name="project",
    )(place, tensor, two_t, three_t)


def turn_kernel(n_terms, *refs):
    terms, (out_ref, turned) = refs[:n_terms], refs[n_terms:]
    total = terms[0][0] if len(terms[0].shape) == 3 else terms[0][...]
    for term in terms[1:]:
        total = total + (term[0] if len(term.shape) == 3 else term[...])
    block, width = total.shape
    lanes = out_ref.shape[1] // (block // 2)
    for unit in range(width // (HALF * lanes)):
        for p in range(HALF):
            at = (unit * HALF + p) * lanes
            for g in range(block // 8):
                turned[pl.ds(g * 8 * HALF + p, 8, stride=HALF), :] = total[g * 8 : g * 8 + 8, at : at + lanes]
        low = lax.broadcasted_iota(jnp.int32, (HALF, lanes), 1) < lanes // 2
        for pair in range(block // 2):
            even = turned[2 * pair * HALF : (2 * pair + 1) * HALF, :]
            odd = turned[(2 * pair + 1) * HALF : (2 * pair + 2) * HALF, :]
            columns = slice(pair * lanes, (pair + 1) * lanes)
            out_ref[unit * UNIT : unit * UNIT + HALF, columns] = jnp.where(low, even, pltpu.roll(odd, lanes // 2, 1))
            out_ref[unit * UNIT + HALF : (unit + 1) * UNIT, columns] = jnp.where(low, pltpu.roll(even, lanes // 2, 1), odd)


def turn(terms, block, rank):
    width = terms[0].shape[-1]
    specs = []
    for term in terms:
        at = term.shape[-2] // block - 1
        if term.ndim == 3:
            specs.append(pl.BlockSpec((1, block, width), lambda i, last=term.shape[0] - 1, at=at: (last, at, 0)))
        else:
            specs.append(pl.BlockSpec((block, width), lambda i, at=at: (at, 0)))
    return pl.pallas_call(
        functools.partial(turn_kernel, len(terms)),
        out_shape=jax.ShapeDtypeStruct((width // rank, block * rank), jnp.float32),
        grid=(1,),
        in_specs=specs,
        out_specs=pl.BlockSpec((width // rank, block * rank), lambda i: (0, 0)),
        scratch_shapes=[pltpu.VMEM((block * HALF, 2 * rank), jnp.float32)],
        name="turn",
    )(*terms)


def split(value):
    high = value.astype(jnp.bfloat16)
    return high, (value - high.astype(jnp.float32)).astype(jnp.bfloat16)


def gram_kernel(place, starts, n_aa, n_col, n_mid, per_core, *refs):
    n_chunks = len(starts)
    rows_in = refs[: n_chunks * n_col]
    others_in = refs[n_chunks * n_col : n_chunks * (n_col + n_aa - 1)]
    out_ref, left, left_low, right, right_low = refs[n_chunks * (n_col + n_aa - 1) :]
    for distance in range(n_col):
        core = place[0] ^ distance
        for k, start in enumerate(starts):
            ref = rows_in[k * n_col + distance]
            for unit in range(ref.shape[0] // UNIT):
                high, low = split(ref[unit * UNIT : (unit + 1) * UNIT, :])
                at = (start + unit) * UNIT
                row = (at // per_core) * n_col * per_core + core * per_core + at % per_core
                where = pl.ds(pl.multiple_of(row, UNIT), UNIT)
                left[where, :], left_low[where, :] = high, low
                if distance == 0:
                    right[0, at : at + UNIT, :], right_low[0, at : at + UNIT, :] = high, low
    for distance in range(1, n_aa):
        for k, start in enumerate(starts):
            ref = others_in[k * (n_aa - 1) + distance - 1]
            where = slice(start * UNIT, start * UNIT + ref.shape[0])
            right[distance, where, :], right_low[distance, where, :] = split(ref[...])
    scale = 1.0 / (n_mid * left.shape[1])
    share = n_mid // n_aa
    dot = functools.partial(
        lax.dot_general, dimension_numbers=(((1,), (1,)), ((), ())), preferred_element_type=jnp.float32
    )
    for distance in range(n_mid):
        goal = place[1] ^ distance
        block = (goal // share) ^ place[2]
        rows = pl.ds(pl.multiple_of((goal % share) * per_core, UNIT), per_core)
        high, low = right[block, rows, :], right_low[block, rows, :]
        value = dot(left[...], high) + (dot(left[...], low) + dot(left_low[...], high))
        out_ref[distance] = value * scale


def gram_terms(place, own, others, starts, n_aa, n_col, n_mid, per_core, local_rows):
    depth = own[0].shape[1]
    held = n_mid // n_aa * per_core
    n_in = len(own) + len(others)
    return pl.pallas_call(
        lambda place, *refs: gram_kernel(place, starts, n_aa, n_col, n_mid, per_core, *refs),
        out_shape=jax.ShapeDtypeStruct((n_mid, local_rows, per_core), jnp.float32),
        in_specs=[pl.BlockSpec(memory_space=pltpu.SMEM)] + [pl.BlockSpec(memory_space=pltpu.VMEM)] * n_in,
        out_specs=pl.BlockSpec(memory_space=pltpu.VMEM),
        scratch_shapes=[pltpu.VMEM((local_rows, depth), jnp.bfloat16)] * 2
        + [pltpu.VMEM((n_aa, held, depth), jnp.bfloat16)] * 2,
        compiler_params=pltpu.CompilerParams(vmem_limit_bytes=40 * 1024 * 1024),
        name="gram_terms",
    )(place, *own, *others)


def body(tensor, factor_two, factor_three):
    n_aa, n_mid, n_col = (lax.axis_size(name) for name in ("aa", "ba", "col"))
    rank = factor_three.shape[1]
    local_rows = tensor.shape[0]
    per_core = local_rows * n_aa // (n_mid * n_col)
    units = local_rows // n_col // UNIT
    bounds = [0]
    for k in range(len(CHUNKS)):
        bounds.append(round(units * sum(CHUNKS[: k + 1]) / sum(CHUNKS)))
    spans = [(a, b) for a, b in zip(bounds, bounds[1:]) if b > a]
    block = rank // n_mid
    place = jnp.stack([lax.axis_index("col"), lax.axis_index("ba"), lax.axis_index("aa")]).astype(jnp.int32)
    two_t, three_t = factor_two.T, factor_three.T

    own, others = [], []
    for first, end in spans:
        product = project(place, tensor, two_t, three_t, first, end - first, n_col, n_mid, per_core)
        terms = [product]
        size = n_col
        for k in range(bits_of(n_col)):
            size //= 2
            send = sum(term[-2 * size : -size] for term in terms)
            terms.append(exchange(send, "col", 1 << k))
        terms = [term[-1] for term in terms]
        size = rank
        for k in range(bits_of(n_mid)):
            size //= 2
            send = sum(term[-2 * size :][:size] for term in terms)
            terms.append(exchange(send, "ba", 1 << k))
        mine = turn(terms, block, rank)
        own += [mine] + [exchange(mine, "col", d) for d in range(1, n_col)]
        others += [exchange(mine, "aa", d) for d in range(1, n_aa)]

    starts = [first for first, _ in spans]
    sums = gram_terms(place, own, others, starts, n_aa, n_col, n_mid, per_core, local_rows)
    gram = sums[0]
    for d in range(1, n_mid):
        gram = gram + exchange(sums[d], "ba", d)
    return gram


def solution(mesh):
    return jax.shard_map(
        body,
        mesh=mesh,
        in_specs=(P("aa", "ba", "col"), P("ba", None), P("col", None)),
        out_specs=P("aa", ("ba", "col")),
        check_vma=False,
    )
```

```python
import functools

import jax
import jax.numpy as jnp
from jax import lax
from jax.experimental import pallas as pl
from jax.experimental.pallas import tpu as pltpu
from jax.sharding import PartitionSpec as P

UNIT = 16
HALF = UNIT // 2
CHUNKS = (3, 3, 2)
VMEM = pl.BlockSpec(memory_space=pltpu.VMEM)
ANY = pl.BlockSpec(memory_space=pl.ANY)
PARAMS = pltpu.CompilerParams(vmem_limit_bytes=40 * 1024 * 1024)
COST = pl.CostEstimate(flops=1, bytes_accessed=1, transcendentals=0)
TOKEN = jax.ShapeDtypeStruct((8, 128), jnp.float32)


def reversed_bits(value, count):
    return sum(((value >> k) & 1) << (count - 1 - k) for k in range(count))


def bits_of(n):
    return n.bit_length() - 1


def exchange(x, axis, distance):
    n = lax.axis_size(axis)
    return lax.ppermute(x, axis, [(i, i ^ distance) for i in range(n)])


def project_kernel(n_mid, per_core, positions, spans, to_hbm, tensor, two_in, three_in, *refs):
    outs, (held, two_ref, three_ref, wide_s, two_s, three_s, sems, *results) = refs[: len(spans)], refs[len(spans) :]
    n_col = lax.axis_size("col")
    rank, n_two = two_ref.shape
    n_three = three_ref.shape[1]
    block = rank // n_mid
    pieces = [(s, p) for s in range(len(spans)) for p in range(len(positions))]

    copies, k = [], 0
    for s, p in pieces:
        core = lax.axis_index("col") ^ reversed_bits(n_col - 1 - positions[p], bits_of(n_col))
        first, count = spans[s]
        copies.append([])
        for at in range(first * UNIT, (first + count) * UNIT, UNIT):
            row = at // per_core * n_col * per_core + core * per_core + at % per_core
            rows = pl.ds(pl.multiple_of(row, UNIT), UNIT)
            copies[-1].append(pltpu.make_async_copy(tensor.at[rows], held.at[k], sems.at[k]))
            copies[-1][-1].start()
            k += 1
        if len(copies) == 1:
            factors = [
                pltpu.make_async_copy(two_in, two_ref, sems.at[sems.shape[0] - 2]),
                pltpu.make_async_copy(three_in, three_ref, sems.at[sems.shape[0] - 1]),
            ]
            for copy in factors:
                copy.start()
    for copy in factors:
        copy.wait()
    wide_s[...] = two_ref[...].astype(jnp.float32)
    blocks = []
    for position in range(n_mid):
        at = lax.axis_index("ba") ^ reversed_bits(n_mid - 1 - position, bits_of(n_mid))
        blocks.append(wide_s[pl.ds(pl.multiple_of(at * block, block), block), :])
    two_s[...] = jnp.concatenate(blocks, axis=0).astype(jnp.bfloat16)
    three = three_ref[...]
    zero = jnp.zeros_like(three)
    three_s[...] = jnp.concatenate(
        [jnp.concatenate([three, zero], axis=1), jnp.concatenate([zero, three], axis=1)], axis=0
    )
    k, flushes = 0, []
    for (s, p), arrivals in zip(pieces, copies):
        count = len(arrivals)
        for copy in arrivals:
            copy.wait()
        values = held[k : k + count]
        k += count
        pairs = jnp.concatenate([values[:, :HALF], values[:, HALF:]], axis=3)
        pairs = pairs.reshape(count * HALF * n_two, 2 * n_three)
        partial_value = lax.dot_general(
            pairs, three_s[...], (((1,), (1,)), ((), ())), preferred_element_type=jnp.float32
        ).astype(jnp.bfloat16)
        partial_value = partial_value.reshape(count * HALF, n_two, 2 * rank)
        wide = jnp.concatenate([partial_value[i] for i in range(count * HALF)], axis=1)
        product = jnp.dot(two_s[...], wide, preferred_element_type=jnp.float32)
        if to_hbm:
            results[s][p] = product
            at = k - count
            flushes.append(pltpu.make_async_copy(results[s].at[p], outs[s].at[p], sems.at[at]))
            flushes[-1].start()
        else:
            outs[s][p] = product
    for copy in flushes:
        copy.wait()


def project(tensor, two_t, three_t, positions, spans, n_mid, per_core, to_hbm):
    n_two, n_three = tensor.shape[1:]
    rank = two_t.shape[0]
    n_units = sum(len(positions) * count for _, count in spans)
    shapes = [(len(positions), rank, count * UNIT * rank) for _, count in spans]
    scratch = [
        pltpu.VMEM((n_units, UNIT, n_two, n_three), jnp.bfloat16),
        pltpu.VMEM((rank, n_two), jnp.bfloat16),
        pltpu.VMEM((rank, n_three), jnp.bfloat16),
        pltpu.VMEM((rank, n_two), jnp.float32),
        pltpu.VMEM((rank, n_two), jnp.bfloat16),
        pltpu.VMEM((2 * rank, 2 * n_three), jnp.bfloat16),
        pltpu.SemaphoreType.DMA((n_units + 2,)),
    ]
    if to_hbm:
        scratch += [pltpu.VMEM(shape, jnp.float32) for shape in shapes]
    return pl.pallas_call(
        functools.partial(project_kernel, n_mid, per_core, positions, spans, to_hbm),
        out_shape=tuple(jax.ShapeDtypeStruct(shape, jnp.float32) for shape in shapes),
        in_specs=[ANY] * 3,
        out_specs=[ANY if to_hbm else VMEM] * len(shapes),
        scratch_shapes=scratch,
        compiler_params=pltpu.CompilerParams(vmem_limit_bytes=(58 if to_hbm else 48) * 1024 * 1024),
        cost_estimate=COST,
        name="project",
    )(tensor, two_t, three_t)


def fold_kernel(keep, got, token, send_out, keep_out, token_out):
    half = keep.shape[0] // 2
    send_out[...] = keep[:half] + got[:half]
    keep_out[...] = keep[half:] + got[half:]
    token_out[...] = token[...]


def fold(keep, got, token):
    half = jax.ShapeDtypeStruct((keep.shape[0] // 2, *keep.shape[1:]), jnp.float32)
    return pl.pallas_call(
        fold_kernel,
        out_shape=(half, half, TOKEN),
        in_specs=[VMEM] * 3,
        out_specs=[VMEM] * 3,
        compiler_params=PARAMS,
        cost_estimate=COST,
        name="fold",
    )(keep, got, token)


def turn_kernel(keep, got, token, out_ref, token_out, turned):
    total = keep[...] + got[...]
    token_out[...] = token[...]
    block, width = total.shape
    lanes = out_ref.shape[1] // (block // 2)
    low = lax.broadcasted_iota(jnp.int32, (HALF, lanes), 1) < lanes // 2
    for unit in range(width // (HALF * lanes)):
        for p in range(HALF):
            at = (unit * HALF + p) * lanes
            for g in range(block // 8):
                turned[unit, pl.ds(g * 8 * HALF + p, 8, stride=HALF), :] = total[g * 8 : g * 8 + 8, at : at + lanes]
        for pair in range(block // 2):
            even = turned[unit, 2 * pair * HALF : (2 * pair + 1) * HALF, :]
            odd = turned[unit, (2 * pair + 1) * HALF : (2 * pair + 2) * HALF, :]
            columns = slice(pair * lanes, (pair + 1) * lanes)
            out_ref[unit * UNIT : unit * UNIT + HALF, columns] = jnp.where(low, even, pltpu.roll(odd, lanes // 2, 1))
            out_ref[unit * UNIT + HALF : (unit + 1) * UNIT, columns] = jnp.where(low, pltpu.roll(even, lanes // 2, 1), odd)


def turn(keep, got, token, rank):
    block, width = keep.shape
    return pl.pallas_call(
        turn_kernel,
        out_shape=(jax.ShapeDtypeStruct((width // rank, block * rank), jnp.float32), TOKEN),
        in_specs=[VMEM] * 3,
        out_specs=[VMEM] * 2,
        scratch_shapes=[pltpu.VMEM((width // rank // UNIT, block * HALF, 2 * rank), jnp.float32)],
        compiler_params=PARAMS,
        cost_estimate=COST,
        name="turn",
    )(keep, got, token)


def split(value):
    high = value.astype(jnp.bfloat16)
    return high, (value - high.astype(jnp.float32)).astype(jnp.bfloat16)


def gram_kernel(starts, n_aa, n_col, n_mid, per_core, *refs):
    place = [lax.axis_index(name) for name in ("col", "ba", "aa")]
    n_chunks = len(starts)
    rows_in = refs[: n_chunks * n_col]
    others_in = refs[n_chunks * n_col : n_chunks * (n_col + n_aa - 1)]
    outs = refs[n_chunks * (n_col + n_aa - 1) : n_chunks * (n_col + n_aa - 1) + n_mid]
    left, left_low, right, right_low = refs[n_chunks * (n_col + n_aa - 1) + n_mid :]
    for distance in range(n_col):
        core = place[0] ^ distance
        for k, start in enumerate(starts):
            ref = rows_in[k * n_col + distance]
            for unit in range(ref.shape[0] // UNIT):
                high, low = split(ref[unit * UNIT : (unit + 1) * UNIT, :])
                at = (start + unit) * UNIT
                row = (at // per_core) * n_col * per_core + core * per_core + at % per_core
                where = pl.ds(pl.multiple_of(row, UNIT), UNIT)
                left[where, :], left_low[where, :] = high, low
                if distance == 0:
                    right[0, at : at + UNIT, :], right_low[0, at : at + UNIT, :] = high, low
    for distance in range(1, n_aa):
        for k, start in enumerate(starts):
            ref = others_in[k * (n_aa - 1) + distance - 1]
            where = slice(start * UNIT, start * UNIT + ref.shape[0])
            right[distance, where, :], right_low[distance, where, :] = split(ref[...])
    scale = 1.0 / (n_mid * left.shape[1])
    share = n_mid // n_aa
    dot = functools.partial(
        lax.dot_general, dimension_numbers=(((1,), (1,)), ((), ())), preferred_element_type=jnp.float32
    )
    for distance in range(n_mid):
        goal = place[1] ^ distance
        block = (goal // share) ^ place[2]
        rows = pl.ds(pl.multiple_of((goal % share) * per_core, UNIT), per_core)
        high, low = right[block, rows, :], right_low[block, rows, :]
        value = dot(left[...], high) + (dot(left[...], low) + dot(left_low[...], high))
        outs[distance][...] = value * scale


def gram_terms(own, others, starts, n_aa, n_col, n_mid, per_core, local_rows):
    depth = own[0].shape[1]
    held = n_mid // n_aa * per_core
    return pl.pallas_call(
        functools.partial(gram_kernel, starts, n_aa, n_col, n_mid, per_core),
        out_shape=(jax.ShapeDtypeStruct((local_rows, per_core), jnp.float32),) * n_mid,
        in_specs=[VMEM] * (len(own) + len(others)),
        out_specs=[VMEM] * n_mid,
        scratch_shapes=[pltpu.VMEM((local_rows, depth), jnp.bfloat16)] * 2
        + [pltpu.VMEM((n_aa, held, depth), jnp.bfloat16)] * 2,
        compiler_params=PARAMS,
        name="gram_terms",
    )(*own, *others)


def body(tensor, factor_two, factor_three):
    n_aa, n_mid, n_col = (lax.axis_size(name) for name in ("aa", "ba", "col"))
    rank = factor_three.shape[1]
    local_rows = tensor.shape[0]
    per_core = local_rows * n_aa // (n_mid * n_col)
    units = local_rows // n_col // UNIT
    bounds = [0]
    for k in range(len(CHUNKS)):
        bounds.append(round(units * sum(CHUNKS[: k + 1]) / sum(CHUNKS)))
    spans = [(a, b - a) for a, b in zip(bounds, bounds[1:]) if b > a]
    n_chunks = len(spans)
    two_t, three_t = factor_two.T, factor_three.T
    token = jnp.zeros(TOKEN.shape, TOKEN.dtype)
    first_half, second_half = tuple(range(n_col // 2)), tuple(range(n_col // 2, n_col))

    sends = project(tensor, two_t, three_t, first_half, spans, n_mid, per_core, True)
    got = [exchange(send, "col", 1) for send in sends]
    keep = list(project(tensor, two_t, three_t, second_half, spans, n_mid, per_core, False))
    mine, own, others = [None] * n_chunks, [], []
    col_steps, mid_steps = bits_of(n_col), bits_of(n_mid)

    def over_col(k, token):
        for step in range(1, col_steps):
            send, keep[k], token = fold(keep[k], got[k], token)
            got[k] = exchange(send, "col", 1 << step)
        keep[k], got[k] = keep[k][0], got[k][0]
        return over_mid(k, 0, token)

    def over_mid(k, step, token):
        send, keep[k], token = fold(keep[k], got[k], token)
        got[k] = exchange(send, "ba", 1 << step)
        return token

    def finish(k, token):
        mine[k], token = turn(keep[k], got[k], token, rank)
        return token

    token = over_col(0, token)
    for k in range(1, n_chunks):
        if k >= 2:
            for step in range(1, mid_steps):
                token = over_mid(k - 2, step, token)
        token = over_col(k, token)
    for k in range(n_chunks):
        if k >= n_chunks - 2:
            for step in range(1, mid_steps):
                token = over_mid(k, step, token)
        if k >= 1:
            token = finish(k - 1, token)
    token = finish(n_chunks - 1, token)
    for k in range(n_chunks):
        own += [mine[k]] + [exchange(mine[k], "col", d) for d in range(1, n_col)]
        others += [exchange(mine[k], "aa", d) for d in range(1, n_aa)]

    starts = [first for first, _ in spans]
    sums = gram_terms(own, others, starts, n_aa, n_col, n_mid, per_core, local_rows)
    gram = sums[0]
    for d in range(1, n_mid):
        gram = gram + exchange(sums[d], "ba", d)
    return gram


def solution(mesh):
    return jax.shard_map(
        body,
        mesh=mesh,
        in_specs=(P("aa", "ba", "col"), P("ba", None), P("col", None)),
        out_specs=P("aa", ("ba", "col")),
        check_vma=False,
    )
```

```python
import functools

import jax
import jax.numpy as jnp
from jax import lax
from jax.experimental import pallas as pl
from jax.experimental.pallas import tpu as pltpu
from jax.sharding import PartitionSpec as P

UNIT = 16
HALF = UNIT // 2
CHUNKS = (3, 3, 2)
ORDER = (
    (("first", 0), ("first", 1), ("later", 0), ("first", 2), ("later", 1)),
    (("finish", 0), ("later", 2), ("finish", 1), ("take", 0), ("finish", 2), ("take", 1), ("take", 2)),
)
VMEM = pl.BlockSpec(memory_space=pltpu.VMEM)
ANY = pl.BlockSpec(memory_space=pl.ANY)
PARAMS = pltpu.CompilerParams(vmem_limit_bytes=40 * 1024 * 1024)
COST = pl.CostEstimate(flops=1, bytes_accessed=1, transcendentals=0)
TOKEN = jax.ShapeDtypeStruct((8, 128), jnp.float32)


def reversed_bits(value, count):
    return sum(((value >> k) & 1) << (count - 1 - k) for k in range(count))


def bits_of(n):
    return n.bit_length() - 1


def exchange(x, axis, distance):
    n = lax.axis_size(axis)
    return lax.ppermute(x, axis, [(i, i ^ distance) for i in range(n)])


def project_kernel(n_mid, per_core, positions, spans, to_hbm, tensor, two_in, three_in, *refs):
    refs = refs if to_hbm else refs[1:]
    outs, (held, two_ref, three_ref, wide_s, two_s, three_s, sems, *results) = refs[: len(spans)], refs[len(spans) :]
    n_col = lax.axis_size("col")
    rank, n_two = two_ref.shape
    n_three = three_ref.shape[1]
    block = rank // n_mid
    pieces = [(s, p) for s in range(len(spans)) for p in range(len(positions))]

    copies, k = [], 0
    for s, p in pieces:
        core = lax.axis_index("col") ^ reversed_bits(n_col - 1 - positions[p], bits_of(n_col))
        first, count = spans[s]
        copies.append([])
        for at in range(first * UNIT, (first + count) * UNIT, UNIT):
            row = at // per_core * n_col * per_core + core * per_core + at % per_core
            rows = pl.ds(pl.multiple_of(row, UNIT), UNIT)
            copies[-1].append(pltpu.make_async_copy(tensor.at[rows], held.at[k], sems.at[k]))
            copies[-1][-1].start()
            k += 1
        if len(copies) == 1:
            factors = [
                pltpu.make_async_copy(two_in, two_ref, sems.at[sems.shape[0] - 2]),
                pltpu.make_async_copy(three_in, three_ref, sems.at[sems.shape[0] - 1]),
            ]
            for copy in factors:
                copy.start()
    for copy in factors:
        copy.wait()
    wide_s[...] = two_ref[...].astype(jnp.float32)
    blocks = []
    for position in range(n_mid):
        at = lax.axis_index("ba") ^ reversed_bits(n_mid - 1 - position, bits_of(n_mid))
        blocks.append(wide_s[pl.ds(pl.multiple_of(at * block, block), block), :])
    two_s[...] = jnp.concatenate(blocks, axis=0).astype(jnp.bfloat16)
    three = three_ref[...]
    zero = jnp.zeros_like(three)
    three_s[...] = jnp.concatenate(
        [jnp.concatenate([three, zero], axis=1), jnp.concatenate([zero, three], axis=1)], axis=0
    )
    k, flushes = 0, []
    for (s, p), arrivals in zip(pieces, copies):
        count = len(arrivals)
        for copy in arrivals:
            copy.wait()
        values = held[k : k + count]
        k += count
        pairs = jnp.concatenate([values[:, :HALF], values[:, HALF:]], axis=3)
        pairs = pairs.reshape(count * HALF * n_two, 2 * n_three)
        partial_value = lax.dot_general(
            pairs, three_s[...], (((1,), (1,)), ((), ())), preferred_element_type=jnp.float32
        ).astype(jnp.bfloat16)
        partial_value = partial_value.reshape(count * HALF, n_two, 2 * rank)
        wide = jnp.concatenate([partial_value[i] for i in range(count * HALF)], axis=1)
        product = jnp.dot(two_s[...], wide, preferred_element_type=jnp.float32)
        if to_hbm:
            results[s][p] = product
            at = k - count
            flushes.append(pltpu.make_async_copy(results[s].at[p], outs[s].at[p], sems.at[at]))
            flushes[-1].start()
        else:
            outs[s][p] = product
    for copy in flushes:
        copy.wait()


def project(tensor, two_t, three_t, token, positions, spans, n_mid, per_core, to_hbm):
    n_two, n_three = tensor.shape[1:]
    rank = two_t.shape[0]
    n_units = sum(len(positions) * count for _, count in spans)
    shapes = [(len(positions), rank, count * UNIT * rank) for _, count in spans]
    scratch = [
        pltpu.VMEM((n_units, UNIT, n_two, n_three), jnp.bfloat16),
        pltpu.VMEM((rank, n_two), jnp.bfloat16),
        pltpu.VMEM((rank, n_three), jnp.bfloat16),
        pltpu.VMEM((rank, n_two), jnp.float32),
        pltpu.VMEM((rank, n_two), jnp.bfloat16),
        pltpu.VMEM((2 * rank, 2 * n_three), jnp.bfloat16),
        pltpu.SemaphoreType.DMA((n_units + 2,)),
    ]
    if to_hbm:
        scratch += [pltpu.VMEM(shape, jnp.float32) for shape in shapes]
    return pl.pallas_call(
        functools.partial(project_kernel, n_mid, per_core, positions, spans, to_hbm),
        out_shape=tuple(jax.ShapeDtypeStruct(shape, jnp.float32) for shape in shapes),
        in_specs=[ANY] * 3 + [VMEM] * (not to_hbm),
        out_specs=[ANY if to_hbm else VMEM] * len(shapes),
        scratch_shapes=scratch,
        compiler_params=pltpu.CompilerParams(vmem_limit_bytes=(58 if to_hbm else 48) * 1024 * 1024),
        cost_estimate=COST,
        name="project",
    )(tensor, two_t, three_t, *(() if to_hbm else (token,)))


def fold_kernel(*refs):
    (keep, got, token), (send_out, keep_out, token_out) = refs[:3], refs[3:]
    half = keep.shape[0] // 2
    send_out[...] = keep[:half] + got[:half]
    keep_out[...] = keep[half:] + got[half:]
    token_out[...] = token[...]


def fold(keep, got, token):
    half = jax.ShapeDtypeStruct((keep.shape[0] // 2, *keep.shape[1:]), jnp.float32)
    return pl.pallas_call(
        fold_kernel,
        out_shape=(half, half, TOKEN),
        in_specs=[VMEM] * 3,
        out_specs=[VMEM] * 3,
        compiler_params=PARAMS,
        cost_estimate=COST,
        name="fold",
    )(keep, got, token)


def deal_kernel(block, keep, got, token, *refs):
    *outs, token_out = refs
    at = 0
    for out in outs:
        out[...] = keep[at : at + out.shape[0]] + got[at : at + out.shape[0]]
        at += out.shape[0]
    token_out[...] = token[...]


def deal(keep, got, token, block):
    blocks, width = keep.shape[0] // block, keep.shape[1]
    half = (blocks + 1) // 2
    sizes = [half - 1, 1, half - 1] + ([1] if blocks % 2 == 0 else [])
    shapes = [jax.ShapeDtypeStruct((size * block, width), jnp.float32) for size in sizes if size]
    *outs, token = pl.pallas_call(
        functools.partial(deal_kernel, block),
        out_shape=(*shapes, TOKEN),
        in_specs=[VMEM] * 3,
        out_specs=[VMEM] * (len(shapes) + 1),
        compiler_params=PARAMS,
        cost_estimate=COST,
        name="deal",
    )(keep, got, token)
    return [outs.pop(0) if size else None for size in sizes], token


def turn_kernel(n_terms, *refs):
    terms, (token, out_ref, token_out, turned) = refs[:n_terms], refs[n_terms:]
    total = sum((term[...] for term in terms[1:]), terms[0][...])
    token_out[...] = token[...]
    block, width = total.shape
    lanes = out_ref.shape[1] // (block // 2)
    low = lax.broadcasted_iota(jnp.int32, (HALF, lanes), 1) < lanes // 2
    for unit in range(width // (HALF * lanes)):
        for p in range(HALF):
            at = (unit * HALF + p) * lanes
            for g in range(block // 8):
                turned[unit, pl.ds(g * 8 * HALF + p, 8, stride=HALF), :] = total[g * 8 : g * 8 + 8, at : at + lanes]
        for pair in range(block // 2):
            even = turned[unit, 2 * pair * HALF : (2 * pair + 1) * HALF, :]
            odd = turned[unit, (2 * pair + 1) * HALF : (2 * pair + 2) * HALF, :]
            columns = slice(pair * lanes, (pair + 1) * lanes)
            out_ref[unit * UNIT : unit * UNIT + HALF, columns] = jnp.where(low, even, pltpu.roll(odd, lanes // 2, 1))
            out_ref[unit * UNIT + HALF : (unit + 1) * UNIT, columns] = jnp.where(low, pltpu.roll(even, lanes // 2, 1), odd)


def turn(terms, token, rank):
    block, width = terms[0].shape
    return pl.pallas_call(
        functools.partial(turn_kernel, len(terms)),
        out_shape=(jax.ShapeDtypeStruct((width // rank, block * rank), jnp.float32), TOKEN),
        in_specs=[VMEM] * (len(terms) + 1),
        out_specs=[VMEM] * 2,
        scratch_shapes=[pltpu.VMEM((width // rank // UNIT, block * HALF, 2 * rank), jnp.float32)],
        compiler_params=PARAMS,
        cost_estimate=COST,
        name="turn",
    )(*terms, token)


def split(value):
    high = value.astype(jnp.bfloat16)
    return high, (value - high.astype(jnp.float32)).astype(jnp.bfloat16)


def absorb_kernel(first, start, n_aa, n_col, n_mid, per_core, last, token, *refs):
    place = [lax.axis_index(name) for name in ("col", "ba", "aa")]
    rows_in, others_in = refs[:n_col], refs[n_col : n_col + n_aa - 1]
    refs = refs[n_col + n_aa - 1 + (0 if first else 4) :]
    left, left_low, right, right_low, token_out, *outs = refs
    token_out[...] = token[...]
    count = rows_in[0].shape[0] // UNIT
    for distance in range(n_col):
        core = place[0] ^ distance
        for unit in range(count):
            high, low = split(rows_in[distance][unit * UNIT : (unit + 1) * UNIT, :])
            at = (start + unit) * UNIT
            row = (at // per_core) * n_col * per_core + core * per_core + at % per_core
            where = pl.ds(pl.multiple_of(row, UNIT), UNIT)
            left[where, :], left_low[where, :] = high, low
            if distance == 0:
                right[0, at : at + UNIT, :], right_low[0, at : at + UNIT, :] = high, low
    for distance in range(1, n_aa):
        where = slice(start * UNIT, (start + count) * UNIT)
        right[distance, where, :], right_low[distance, where, :] = split(others_in[distance - 1][...])
    if not last:
        return
    scale = 1.0 / (n_mid * left.shape[1])
    share = n_mid // n_aa
    dot = functools.partial(
        lax.dot_general, dimension_numbers=(((1,), (1,)), ((), ())), preferred_element_type=jnp.float32
    )
    for distance in range(n_mid):
        goal = place[1] ^ distance
        block = (goal // share) ^ place[2]
        rows = pl.ds(pl.multiple_of((goal % share) * per_core, UNIT), per_core)
        high, low = right[block, rows, :], right_low[block, rows, :]
        value = dot(left[...], high) + (dot(left[...], low) + dot(left_low[...], high))
        outs[distance][...] = value * scale


def absorb(token, rows, others, held, start, n_aa, n_col, n_mid, per_core, local_rows, last):
    depth = rows[0].shape[1]
    shapes = [jax.ShapeDtypeStruct((local_rows, depth), jnp.bfloat16)] * 2
    shapes += [jax.ShapeDtypeStruct((n_aa, n_mid // n_aa * per_core, depth), jnp.bfloat16)] * 2
    shapes += [TOKEN] + [jax.ShapeDtypeStruct((local_rows, per_core), jnp.float32)] * (n_mid if last else 0)
    n_in = 1 + len(rows) + len(others)
    outs = pl.pallas_call(
        functools.partial(absorb_kernel, not held, start, n_aa, n_col, n_mid, per_core, last),
        out_shape=tuple(shapes),
        in_specs=[VMEM] * (n_in + len(held)),
        out_specs=[VMEM] * len(shapes),
        input_output_aliases={n_in + i: i for i in range(len(held))},
        compiler_params=PARAMS,
        cost_estimate=COST,
        name="gram" if last else "absorb",
    )(token, *rows, *others, *held)
    return outs[:4], outs[4], outs[5:]


def body(tensor, factor_two, factor_three):
    n_aa, n_mid, n_col = (lax.axis_size(name) for name in ("aa", "ba", "col"))
    rank = factor_three.shape[1]
    local_rows = tensor.shape[0]
    per_core = local_rows * n_aa // (n_mid * n_col)
    units = local_rows // n_col // UNIT
    bounds = [0]
    for k in range(len(CHUNKS)):
        bounds.append(round(units * sum(CHUNKS[: k + 1]) / sum(CHUNKS)))
    spans = [(a, b - a) for a, b in zip(bounds, bounds[1:]) if b > a]
    n_chunks = len(spans)
    block = rank // n_mid
    two_t, three_t = factor_two.T, factor_three.T
    token = jnp.zeros(TOKEN.shape, TOKEN.dtype)
    first_half, second_half = tuple(range(n_col // 2)), tuple(range(n_col // 2, n_col))

    sends = project(tensor, two_t, three_t, token, first_half, spans, n_mid, per_core, True)
    got = [exchange(send, "col", 1) for send in sends]
    keep = list(project(tensor, two_t, three_t, token, second_half, spans[:1], n_mid, per_core, False))
    col_steps, mid_steps = bits_of(n_col), bits_of(n_mid)
    finals, gathered = [[] for _ in spans], [None] * n_chunks
    held = ()

    def first_step(k, token):
        for step in range(1, col_steps):
            send, keep[k], token = fold(keep[k], got[k], token)
            got[k] = exchange(send, "col", 1 << step)
        (onward, final, keep[k], mine), token = deal(keep[k][0], got[k][0], token, block)
        got[k] = exchange(onward, "ba", 1)
        if k == 0 and spans[1:]:
            keep.extend(project(tensor, two_t, three_t, token, second_half, spans[1:], n_mid, per_core, False))
        finals[k] += [mine, exchange(final, "ba", 1)]
        return token

    def later_steps(k, token):
        for step in range(1, mid_steps):
            (onward, final, keep[k]), token = deal(keep[k], got[k], token, block)
            if onward is not None:
                got[k] = exchange(onward, "ba", 1 << step)
            finals[k].append(exchange(final, "ba", 1 << step))
        return token

    def finish(k, token):
        mine, token = turn(finals[k], token, rank)
        rows = [mine] + [exchange(mine, "col", d) for d in range(1, n_col)]
        gathered[k] = rows, [exchange(mine, "aa", d) for d in range(1, n_aa)]
        return token

    def take(k, token, held):
        last = k == n_chunks - 1
        return absorb(token, *gathered[k], held, spans[k][0], n_aa, n_col, n_mid, per_core, local_rows, last)

    for order in ORDER:
        for name, k in order:
            if k >= n_chunks:
                continue
            if name == "first":
                token = first_step(k, token)
            elif name == "later":
                token = later_steps(k, token)
            elif name == "finish":
                token = finish(k, token)
            else:
                held, token, sums = take(k, token, held)
    gram = sums[0]
    for d in range(1, n_mid):
        gram = gram + exchange(sums[d], "ba", d)
    return gram


def solution(mesh):
    return jax.shard_map(
        body,
        mesh=mesh,
        in_specs=(P("aa", "ba", "col"), P("ba", None), P("col", None)),
        out_specs=P("aa", ("ba", "col")),
        check_vma=False,
    )
```

```python
import functools

import jax
import jax.numpy as jnp
from jax import lax
from jax.experimental import pallas as pl
from jax.experimental.pallas import tpu as pltpu
from jax.sharding import PartitionSpec as P

UNIT = 16
HALF = UNIT // 2
CHUNKS = (3, 3, 2)
ORDER = (
    (("first", 0), ("first", 1), ("later", 0), ("first", 2), ("later", 1)),
    (("finish", 0), ("later", 2), ("finish", 1), ("take", 0), ("finish", 2), ("take", 1), ("take", 2)),
)
CORE = {0: (0,), 1: (1,), 2: (2,)}
WHOLE = ()
LATE = ()
SOON = (1,)
SUMS = (2, 3, 1)
VMEM = pl.BlockSpec(memory_space=pltpu.VMEM)
ANY = pl.BlockSpec(memory_space=pl.ANY)
PARAMS = pltpu.CompilerParams(vmem_limit_bytes=40 * 1024 * 1024)
COST = pl.CostEstimate(flops=1, bytes_accessed=1, transcendentals=0)
TOKEN = jax.ShapeDtypeStruct((8, 128), jnp.float32)


def reversed_bits(value, count):
    return sum(((value >> k) & 1) << (count - 1 - k) for k in range(count))


def bits_of(n):
    return n.bit_length() - 1


def exchange(x, axis, distance):
    n = lax.axis_size(axis)
    return lax.ppermute(x, axis, [(i, i ^ distance) for i in range(n)])


def project_kernel(n_mid, per_core, positions, spans, to_hbm, tensor, two_in, three_in, *refs):
    refs = refs if to_hbm else refs[1:]
    outs, (held, two_ref, three_ref, wide_s, two_s, three_s, sems, *results) = refs[: len(spans)], refs[len(spans) :]
    n_col = lax.axis_size("col")
    rank, n_two = two_ref.shape
    n_three = three_ref.shape[1]
    block = rank // n_mid
    pieces = [(s, p) for s in range(len(spans)) for p in range(len(positions))]

    copies, k = [], 0
    for s, p in pieces:
        core = lax.axis_index("col") ^ reversed_bits(n_col - 1 - positions[p], bits_of(n_col))
        first, count = spans[s]
        copies.append([])
        for at in range(first * UNIT, (first + count) * UNIT, UNIT):
            row = at // per_core * n_col * per_core + core * per_core + at % per_core
            rows = pl.ds(pl.multiple_of(row, UNIT), UNIT)
            copies[-1].append(pltpu.make_async_copy(tensor.at[rows], held.at[k], sems.at[k]))
            copies[-1][-1].start()
            k += 1
        if len(copies) == 1:
            factors = [
                pltpu.make_async_copy(two_in, two_ref, sems.at[sems.shape[0] - 2]),
                pltpu.make_async_copy(three_in, three_ref, sems.at[sems.shape[0] - 1]),
            ]
            for copy in factors:
                copy.start()
    for copy in factors:
        copy.wait()
    wide_s[...] = two_ref[...].astype(jnp.float32)
    blocks = []
    for position in range(n_mid):
        at = lax.axis_index("ba") ^ reversed_bits(n_mid - 1 - position, bits_of(n_mid))
        blocks.append(wide_s[pl.ds(pl.multiple_of(at * block, block), block), :])
    two_s[...] = jnp.concatenate(blocks, axis=0).astype(jnp.bfloat16)
    three = three_ref[...]
    zero = jnp.zeros_like(three)
    three_s[...] = jnp.concatenate(
        [jnp.concatenate([three, zero], axis=1), jnp.concatenate([zero, three], axis=1)], axis=0
    )
    k, flushes = 0, []
    for (s, p), arrivals in zip(pieces, copies):
        count = len(arrivals)
        for copy in arrivals:
            copy.wait()
        values = held[k : k + count]
        k += count
        pairs = jnp.concatenate([values[:, :HALF], values[:, HALF:]], axis=3)
        pairs = pairs.reshape(count * HALF * n_two, 2 * n_three)
        partial_value = lax.dot_general(
            pairs, three_s[...], (((1,), (1,)), ((), ())), preferred_element_type=jnp.float32
        ).astype(jnp.bfloat16)
        partial_value = partial_value.reshape(count * HALF, n_two, 2 * rank)
        wide = jnp.concatenate([partial_value[i] for i in range(count * HALF)], axis=1)
        product = jnp.dot(two_s[...], wide, preferred_element_type=jnp.float32)
        if to_hbm:
            results[s][p] = product
            at = k - count
            flushes.append(pltpu.make_async_copy(results[s].at[p], outs[s].at[p], sems.at[at]))
            flushes[-1].start()
        else:
            outs[s][p] = product
    for copy in flushes:
        copy.wait()


def project(tensor, two_t, three_t, token, positions, spans, n_mid, per_core, to_hbm):
    n_two, n_three = tensor.shape[1:]
    rank = two_t.shape[0]
    n_units = sum(len(positions) * count for _, count in spans)
    shapes = [(len(positions), rank, count * UNIT * rank) for _, count in spans]
    scratch = [
        pltpu.VMEM((n_units, UNIT, n_two, n_three), jnp.bfloat16),
        pltpu.VMEM((rank, n_two), jnp.bfloat16),
        pltpu.VMEM((rank, n_three), jnp.bfloat16),
        pltpu.VMEM((rank, n_two), jnp.float32),
        pltpu.VMEM((rank, n_two), jnp.bfloat16),
        pltpu.VMEM((2 * rank, 2 * n_three), jnp.bfloat16),
        pltpu.SemaphoreType.DMA((n_units + 2,)),
    ]
    if to_hbm:
        scratch += [pltpu.VMEM(shape, jnp.float32) for shape in shapes]
    return pl.pallas_call(
        functools.partial(project_kernel, n_mid, per_core, positions, spans, to_hbm),
        out_shape=tuple(jax.ShapeDtypeStruct(shape, jnp.float32) for shape in shapes),
        in_specs=[ANY] * 3 + [VMEM] * (not to_hbm),
        out_specs=[ANY if to_hbm else VMEM] * len(shapes),
        scratch_shapes=scratch,
        compiler_params=pltpu.CompilerParams(vmem_limit_bytes=(58 if to_hbm else 48) * 1024 * 1024),
        cost_estimate=COST,
        name="project",
    )(tensor, two_t, three_t, *(() if to_hbm else (token,)))


def fold_kernel(*refs):
    (keep, got, token), (send_out, keep_out, token_out) = refs[:3], refs[3:]
    half = keep.shape[0] // 2
    send_out[...] = keep[:half] + got[:half]
    keep_out[...] = keep[half:] + got[half:]
    token_out[...] = token[...]


def fold(keep, got, token):
    half = jax.ShapeDtypeStruct((keep.shape[0] // 2, *keep.shape[1:]), jnp.float32)
    return pl.pallas_call(
        fold_kernel,
        out_shape=(half, half, TOKEN),
        in_specs=[VMEM] * 3,
        out_specs=[VMEM] * 3,
        compiler_params=PARAMS,
        cost_estimate=COST,
        name="fold",
    )(keep, got, token)


def deal_kernel(block, n_through, n_after, keep, got, token, *refs):
    through, (*outs, token_out) = refs[:n_through], refs[n_through + n_after :]
    if through:
        outs.pop()[...] = through[0][...]
    at = 0
    for out in outs:
        out[...] = keep[at : at + out.shape[0]] + got[at : at + out.shape[0]]
        at += out.shape[0]
    token_out[...] = token[...]


def deal(keep, got, token, after, block, through=()):
    blocks, width = keep.shape[0] // block, keep.shape[1]
    half = (blocks + 1) // 2
    sizes = [half - 1, 1, half - 1] + ([1] if blocks % 2 == 0 else [])
    shapes = [jax.ShapeDtypeStruct((size * block, width), jnp.float32) for size in sizes if size]
    shapes += [jax.ShapeDtypeStruct(t.shape, t.dtype) for t in through]
    *outs, token = pl.pallas_call(
        functools.partial(deal_kernel, block, len(through), len(after)),
        out_shape=(*shapes, TOKEN),
        in_specs=[VMEM] * (3 + len(through) + len(after)),
        out_specs=[VMEM] * (len(shapes) + 1),
        compiler_params=PARAMS,
        cost_estimate=COST,
        name="deal",
    )(keep, got, token, *through, *after)
    return [outs.pop(0) if size else None for size in sizes], token, outs


def turn_kernel(n_terms, n_earlier, copied, n_after, *refs):
    refs = refs[n_after:]
    terms, earlier, (token, out_ref, token_out, *joined, turned) = refs[:n_terms], refs[n_terms : n_terms + n_earlier], refs[n_terms + n_earlier :]
    total = sum((term[...] for term in terms[1:]), terms[0][...])
    turn_rows(total, out_ref, turned)
    if copied:
        copies = joined.pop()
        for k in range(copies.shape[0]):
            copies[k] = out_ref[...]
    row = 0
    for ref in (*earlier, out_ref) if joined else ():
        joined[0][row : row + ref.shape[0], :] = ref[...]
        row += ref.shape[0]
    token_out[...] = token[...]


def turn_rows(total, out_ref, turned):
    block, width = total.shape
    lanes = out_ref.shape[1] // (block // 2)
    low = lax.broadcasted_iota(jnp.int32, (HALF, lanes), 1) < lanes // 2
    for unit in range(width // (HALF * lanes)):
        for p in range(HALF):
            at = (unit * HALF + p) * lanes
            for g in range(block // 8):
                turned[unit, pl.ds(g * 8 * HALF + p, 8, stride=HALF), :] = total[g * 8 : g * 8 + 8, at : at + lanes]
        for pair in range(block // 2):
            even = turned[unit, 2 * pair * HALF : (2 * pair + 1) * HALF, :]
            odd = turned[unit, (2 * pair + 1) * HALF : (2 * pair + 2) * HALF, :]
            columns = slice(pair * lanes, (pair + 1) * lanes)
            out_ref[unit * UNIT : unit * UNIT + HALF, columns] = jnp.where(low, even, pltpu.roll(odd, lanes // 2, 1))
            out_ref[unit * UNIT + HALF : (unit + 1) * UNIT, columns] = jnp.where(low, pltpu.roll(even, lanes // 2, 1), odd)


def turn(terms, earlier, copies, token, after, rank):
    block, width = terms[0].shape
    shapes = [jax.ShapeDtypeStruct((width // rank, block * rank), jnp.float32), TOKEN]
    if earlier:
        rows = width // rank + sum(e.shape[0] for e in earlier)
        shapes.append(jax.ShapeDtypeStruct((rows, block * rank), jnp.float32))
    if copies:
        shapes.append(jax.ShapeDtypeStruct((copies, width // rank, block * rank), jnp.float32))
    return pl.pallas_call(
        functools.partial(turn_kernel, len(terms), len(earlier), copies > 0, len(after)),
        out_shape=tuple(shapes),
        in_specs=[VMEM] * (len(terms) + len(earlier) + len(after) + 1),
        out_specs=[VMEM] * len(shapes),
        scratch_shapes=[pltpu.VMEM((width // rank // UNIT, block * HALF, 2 * rank), jnp.float32)],
        compiler_params=PARAMS,
        cost_estimate=COST,
        name="turn",
    )(*after, *terms, *earlier, token)


def split(value):
    high = value.astype(jnp.bfloat16)
    return high, (value - high.astype(jnp.float32)).astype(jnp.bfloat16)


def absorb_kernel(first, start, rows_start, n_others, n_aa, n_col, n_mid, per_core, last, n_after, token, mine, *refs):
    refs = refs[n_after:]
    place = [lax.axis_index(name) for name in ("col", "ba", "aa")]
    n_rows = 0 if rows_start is None else n_col - 1
    rows_in, others_in = refs[:n_rows], refs[n_rows : n_others + n_rows]
    refs = refs[n_others + n_rows + (0 if first else 4) :]
    left, left_low, right, right_low, token_out, *outs = refs
    token_out[...] = token[...]
    count = mine.shape[0] // UNIT

    def put_left(unit, core, high, low):
        at = unit * UNIT
        row = (at // per_core) * n_col * per_core + core * per_core + at % per_core
        where = pl.ds(pl.multiple_of(row, UNIT), UNIT)
        left[where, :], left_low[where, :] = high, low

    for unit in range(count):
        high, low = split(mine[unit * UNIT : (unit + 1) * UNIT, :])
        put_left(start + unit, place[0], high, low)
        where = slice((start + unit) * UNIT, (start + unit + 1) * UNIT)
        right[0, where, :], right_low[0, where, :] = high, low
    for i, distance in enumerate(range(1, n_aa)):
        where = slice(start * UNIT, (start + count) * UNIT)
        right[distance, where, :], right_low[distance, where, :] = split(
            others_in[0][place[2] ^ distance] if n_others == 1 else others_in[i][...]
        )
    for distance in range(1, n_rows + 1):
        ref = rows_in[distance - 1]
        for unit in range(ref.shape[0] // UNIT):
            put_left(rows_start + unit, place[0] ^ distance, *split(ref[unit * UNIT : (unit + 1) * UNIT, :]))
    if not last:
        return
    scale = 1.0 / (n_mid * left.shape[1])
    share = n_mid // n_aa
    dot = functools.partial(
        lax.dot_general, dimension_numbers=(((1,), (1,)), ((), ())), preferred_element_type=jnp.float32
    )
    for distance in range(n_mid):
        goal = place[1] ^ distance
        block = (goal // share) ^ place[2]
        rows = pl.ds(pl.multiple_of((goal % share) * per_core, UNIT), per_core)
        high, low = right[block, rows, :], right_low[block, rows, :]
        value = dot(left[...], high) + (dot(left[...], low) + dot(left_low[...], high))
        outs[distance][...] = value * scale


def absorb(token, after, mine, others, rows, held, start, rows_start, n_aa, n_col, n_mid, per_core, local_rows, last):
    depth = mine.shape[1]
    shapes = [jax.ShapeDtypeStruct((local_rows, depth), jnp.bfloat16)] * 2
    shapes += [jax.ShapeDtypeStruct((n_aa, n_mid // n_aa * per_core, depth), jnp.bfloat16)] * 2
    shapes += [TOKEN] + [jax.ShapeDtypeStruct((local_rows, per_core), jnp.float32)] * (n_mid if last else 0)
    n_in = 2 + len(after) + len(others) + len(rows)
    outs = pl.pallas_call(
        functools.partial(absorb_kernel, not held, start, rows_start, len(others), n_aa, n_col, n_mid, per_core, last, len(after)),
        out_shape=tuple(shapes),
        in_specs=[VMEM] * (n_in + len(held)),
        out_specs=[VMEM] * len(shapes),
        input_output_aliases={n_in + i: i for i in range(len(held))},
        compiler_params=PARAMS,
        cost_estimate=COST,
        name="gram" if last else "absorb",
    )(token, mine, *after, *rows, *others, *held)
    return outs[:4], outs[4], outs[5:]


def body(tensor, factor_two, factor_three):
    n_aa, n_mid, n_col = (lax.axis_size(name) for name in ("aa", "ba", "col"))
    rank = factor_three.shape[1]
    local_rows = tensor.shape[0]
    per_core = local_rows * n_aa // (n_mid * n_col)
    units = local_rows // n_col // UNIT
    bounds = [0]
    for k in range(len(CHUNKS)):
        bounds.append(round(units * sum(CHUNKS[: k + 1]) / sum(CHUNKS)))
    spans = [(a, b - a) for a, b in zip(bounds, bounds[1:]) if b > a]
    n_chunks = len(spans)
    block = rank // n_mid
    two_t, three_t = factor_two.T, factor_three.T
    token = jnp.zeros(TOKEN.shape, TOKEN.dtype)
    first_half, second_half = tuple(range(n_col // 2)), tuple(range(n_col // 2, n_col))

    sends = project(tensor, two_t, three_t, token, first_half, spans, n_mid, per_core, True)
    got = [exchange(send, "col", 1) for send in sends]
    keep = list(project(tensor, two_t, three_t, token, second_half, spans[:1], n_mid, per_core, False))
    col_steps, mid_steps = bits_of(n_col), bits_of(n_mid)
    finals, gathered = [[] for _ in spans], [None] * n_chunks
    held, mine, rows, shared, waiting, after = (), {}, {}, set(), {}, []

    def take_after():
        taken = list(after)
        after.clear()
        return taken

    def first_step(k, token):
        for step in range(1, col_steps):
            send, keep[k], token = fold(keep[k], got[k], token)
            got[k] = exchange(send, "col", 1 << step)
        (onward, final, keep[k], own), token, _ = deal(keep[k][0], got[k][0], token, take_after(), block)
        got[k] = exchange(onward, "ba", 1)
        if k == 0 and spans[1:]:
            keep.extend(project(tensor, two_t, three_t, token, second_half, spans[1:], n_mid, per_core, False))
        finals[k].append(own)
        if k in LATE:
            waiting[k] = [final]
        else:
            finals[k].append(exchange(final, "ba", 1))
        return token

    def later_steps(k, token):
        for step in range(1, mid_steps):
            (onward, final, keep[k]), token, late = deal(keep[k], got[k], token, take_after(), block, waiting.pop(k, []))
            finals[k] += [exchange(block_late, "ba", 1) for block_late in late]
            if onward is not None:
                got[k] = exchange(onward, "ba", 1 << step)
            finals[k].append(exchange(final, "ba", 1 << step))
        return token

    def finish(k, token):
        last = k == n_chunks - 1
        sent = [c for c in CORE.get(k, ()) if c < k] if k < max(CORE) else []
        sent = [c for c in range(k) if c not in shared] if last else sent
        copies = n_aa if k in WHOLE else 0
        out, token, *joined = turn(finals[k], [mine[c] for c in sent], copies, token, take_after(), rank)
        mine[k] = out
        def gather():
            if copies:
                gathered[k] = [lax.all_to_all(joined.pop(), "aa", 0, 0, tiled=True)]
            else:
                gathered[k] = [exchange(out, "aa", d) for d in range(1, n_aa)]

        source = joined[0] if sent else out
        if last or k in CORE.get(k, ()):
            shared.update(sent + [k])
            rows[k] = [exchange(source, "col", d) for d in range(1, n_col)], spans[min(sent + [k])][0]
            if k in SOON:
                after.extend(rows[k][0])
        gather()
        return token

    def take(k, token, held):
        last = k == n_chunks - 1
        others, (came, rows_start) = gathered[k], rows.get(k, ([], None))
        return absorb(
            token, take_after(), mine[k], others, came, held, spans[k][0], rows_start, n_aa, n_col, n_mid, per_core, local_rows, last
        )

    for order in ORDER:
        for name, k in order:
            if k >= n_chunks:
                continue
            if name == "first":
                token = first_step(k, token)
            elif name == "later":
                token = later_steps(k, token)
            elif name == "finish":
                token = finish(k, token)
            else:
                held, token, sums = take(k, token, held)
    gram = sums[0]
    for d in SUMS if n_mid == 4 else range(1, n_mid):
        gram = gram + exchange(sums[d], "ba", d)
    return gram


def solution(mesh):
    return jax.shard_map(
        body,
        mesh=mesh,
        in_specs=(P("aa", "ba", "col"), P("ba", None), P("col", None)),
        out_specs=P("aa", ("ba", "col")),
        check_vma=False,
    )
```

```python
import functools

import jax
import jax.numpy as jnp
from jax import lax
from jax.experimental import pallas as pl
from jax.experimental.pallas import tpu as pltpu
from jax.sharding import PartitionSpec as P

UNIT = 16
HALF = UNIT // 2
CHUNKS = (3, 3, 2)
ORDER = (
    (("first", 0), ("first", 1), ("later", 0), ("first", 2), ("later", 1)),
    (("finish", 0), ("later", 2), ("finish", 1), ("take", 0), ("finish", 2), ("take", 1), ("take", 2)),
)
CORE = {0: (0,), 1: (1,), 2: (2,)}
WHOLE = ()
LATE = ()
SOON = (1,)
SUMS = (2, 3, 1)
VMEM = pl.BlockSpec(memory_space=pltpu.VMEM)
ANY = pl.BlockSpec(memory_space=pl.ANY)
PARAMS = pltpu.CompilerParams(vmem_limit_bytes=40 * 1024 * 1024)
COST = pl.CostEstimate(flops=1, bytes_accessed=1, transcendentals=0)
TOKEN = jax.ShapeDtypeStruct((8, 128), jnp.float32)


def reversed_bits(value, count):
    return sum(((value >> k) & 1) << (count - 1 - k) for k in range(count))


def bits_of(n):
    return n.bit_length() - 1


def exchange(x, axis, distance):
    n = lax.axis_size(axis)
    return lax.ppermute(x, axis, [(i, i ^ distance) for i in range(n)])


def project_kernel(n_mid, per_core, positions, spans, to_hbm, tensor, two_in, three_in, *refs):
    refs = refs if to_hbm else refs[1:]
    outs, (held, two_ref, three_ref, wide_s, two_s, three_s, sems, *results) = refs[: len(spans)], refs[len(spans) :]
    n_col = lax.axis_size("col")
    rank, n_two = two_ref.shape
    n_three = three_ref.shape[1]
    block = rank // n_mid
    pieces = [(s, p) for s in range(len(spans)) for p in range(len(positions))]

    copies, k = [], 0
    for s, p in pieces:
        core = lax.axis_index("col") ^ reversed_bits(n_col - 1 - positions[p], bits_of(n_col))
        first, count = spans[s]
        copies.append([])
        for at in range(first * UNIT, (first + count) * UNIT, UNIT):
            row = at // per_core * n_col * per_core + core * per_core + at % per_core
            rows = pl.ds(pl.multiple_of(row, UNIT), UNIT)
            copies[-1].append(pltpu.make_async_copy(tensor.at[rows], held.at[k], sems.at[k]))
            copies[-1][-1].start()
            k += 1
        if len(copies) == 1:
            factors = [
                pltpu.make_async_copy(two_in, two_ref, sems.at[sems.shape[0] - 2]),
                pltpu.make_async_copy(three_in, three_ref, sems.at[sems.shape[0] - 1]),
            ]
            for copy in factors:
                copy.start()
    for copy in factors:
        copy.wait()
    wide_s[...] = two_ref[...].astype(jnp.float32)
    blocks = []
    for position in range(n_mid):
        at = lax.axis_index("ba") ^ reversed_bits(n_mid - 1 - position, bits_of(n_mid))
        blocks.append(wide_s[pl.ds(pl.multiple_of(at * block, block), block), :])
    two_s[...] = jnp.concatenate(blocks, axis=0).astype(jnp.bfloat16)
    three = three_ref[...]
    zero = jnp.zeros_like(three)
    three_s[...] = jnp.concatenate(
        [jnp.concatenate([three, zero], axis=1), jnp.concatenate([zero, three], axis=1)], axis=0
    )
    k, flushes = 0, []
    for (s, p), arrivals in zip(pieces, copies):
        count = len(arrivals)
        for copy in arrivals:
            copy.wait()
        values = held[k : k + count]
        k += count
        pairs = jnp.concatenate([values[:, :HALF], values[:, HALF:]], axis=3)
        pairs = pairs.reshape(count * HALF * n_two, 2 * n_three)
        partial_value = lax.dot_general(
            pairs, three_s[...], (((1,), (1,)), ((), ())), preferred_element_type=jnp.float32
        ).astype(jnp.bfloat16)
        partial_value = partial_value.reshape(count * HALF, n_two, 2 * rank)
        wide = jnp.concatenate([partial_value[i] for i in range(count * HALF)], axis=1)
        product = jnp.dot(two_s[...], wide, preferred_element_type=jnp.float32)
        if to_hbm:
            results[s][p] = product
            at = k - count
            flushes.append(pltpu.make_async_copy(results[s].at[p], outs[s].at[p], sems.at[at]))
            flushes[-1].start()
        else:
            outs[s][p] = product
    for copy in flushes:
        copy.wait()


def project(tensor, two_t, three_t, token, positions, spans, n_mid, per_core, to_hbm):
    n_two, n_three = tensor.shape[1:]
    rank = two_t.shape[0]
    n_units = sum(len(positions) * count for _, count in spans)
    shapes = [(len(positions), rank, count * UNIT * rank) for _, count in spans]
    scratch = [
        pltpu.VMEM((n_units, UNIT, n_two, n_three), jnp.bfloat16),
        pltpu.VMEM((rank, n_two), jnp.bfloat16),
        pltpu.VMEM((rank, n_three), jnp.bfloat16),
        pltpu.VMEM((rank, n_two), jnp.float32),
        pltpu.VMEM((rank, n_two), jnp.bfloat16),
        pltpu.VMEM((2 * rank, 2 * n_three), jnp.bfloat16),
        pltpu.SemaphoreType.DMA((n_units + 2,)),
    ]
    if to_hbm:
        scratch += [pltpu.VMEM(shape, jnp.float32) for shape in shapes]
    return pl.pallas_call(
        functools.partial(project_kernel, n_mid, per_core, positions, spans, to_hbm),
        out_shape=tuple(jax.ShapeDtypeStruct(shape, jnp.float32) for shape in shapes),
        in_specs=[ANY] * 3 + [VMEM] * (not to_hbm),
        out_specs=[ANY if to_hbm else VMEM] * len(shapes),
        scratch_shapes=scratch,
        compiler_params=pltpu.CompilerParams(vmem_limit_bytes=(58 if to_hbm else 48) * 1024 * 1024),
        cost_estimate=COST,
        name="project",
    )(tensor, two_t, three_t, *(() if to_hbm else (token,)))


def fold_kernel(*refs):
    (keep, got, token), (send_out, keep_out, token_out) = refs[:3], refs[3:]
    half = keep.shape[0] // 2
    send_out[...] = keep[:half] + got[:half]
    keep_out[...] = keep[half:] + got[half:]
    token_out[...] = token[...]


def fold(keep, got, token):
    half = jax.ShapeDtypeStruct((keep.shape[0] // 2, *keep.shape[1:]), jnp.float32)
    return pl.pallas_call(
        fold_kernel,
        out_shape=(half, half, TOKEN),
        in_specs=[VMEM] * 3,
        out_specs=[VMEM] * 3,
        compiler_params=PARAMS,
        cost_estimate=COST,
        name="fold",
    )(keep, got, token)


def deal_kernel(block, n_through, n_after, keep, got, token, *refs):
    through, (*outs, token_out) = refs[:n_through], refs[n_through + n_after :]
    if through:
        outs.pop()[...] = through[0][...]
    at = 0
    for out in outs:
        out[...] = keep[at : at + out.shape[0]] + got[at : at + out.shape[0]]
        at += out.shape[0]
    token_out[...] = token[...]


def deal(keep, got, token, after, block, through=()):
    blocks, width = keep.shape[0] // block, keep.shape[1]
    half = (blocks + 1) // 2
    sizes = [half - 1, 1, half - 1] + ([1] if blocks % 2 == 0 else [])
    shapes = [jax.ShapeDtypeStruct((size * block, width), jnp.float32) for size in sizes if size]
    shapes += [jax.ShapeDtypeStruct(t.shape, t.dtype) for t in through]
    *outs, token = pl.pallas_call(
        functools.partial(deal_kernel, block, len(through), len(after)),
        out_shape=(*shapes, TOKEN),
        in_specs=[VMEM] * (3 + len(through) + len(after)),
        out_specs=[VMEM] * (len(shapes) + 1),
        compiler_params=PARAMS,
        cost_estimate=COST,
        name="deal",
    )(keep, got, token, *through, *after)
    return [outs.pop(0) if size else None for size in sizes], token, outs


def turn_kernel(n_terms, n_earlier, copied, n_after, *refs):
    refs = refs[n_after:]
    terms, earlier, (token, out_ref, token_out, *joined, turned) = refs[:n_terms], refs[n_terms : n_terms + n_earlier], refs[n_terms + n_earlier :]
    total = sum((term[...] for term in terms[1:]), terms[0][...])
    turn_rows(total, out_ref, turned)
    if copied:
        copies = joined.pop()
        for k in range(copies.shape[0]):
            copies[k] = out_ref[...]
    row = 0
    for ref in (*earlier, out_ref) if joined else ():
        joined[0][row : row + ref.shape[0], :] = ref[...]
        row += ref.shape[0]
    token_out[...] = token[...]


def turn_rows(total, out_ref, turned):
    block, width = total.shape
    lanes = out_ref.shape[1] // (block // 2)
    low = lax.broadcasted_iota(jnp.int32, (HALF, lanes), 1) < lanes // 2
    for unit in range(width // (HALF * lanes)):
        for p in range(HALF):
            at = (unit * HALF + p) * lanes
            for g in range(block // 8):
                turned[unit, pl.ds(g * 8 * HALF + p, 8, stride=HALF), :] = total[g * 8 : g * 8 + 8, at : at + lanes]
        for pair in range(block // 2):
            even = turned[unit, 2 * pair * HALF : (2 * pair + 1) * HALF, :]
            odd = turned[unit, (2 * pair + 1) * HALF : (2 * pair + 2) * HALF, :]
            columns = slice(pair * lanes, (pair + 1) * lanes)
            out_ref[unit * UNIT : unit * UNIT + HALF, columns] = jnp.where(low, even, pltpu.roll(odd, lanes // 2, 1))
            out_ref[unit * UNIT + HALF : (unit + 1) * UNIT, columns] = jnp.where(low, pltpu.roll(even, lanes // 2, 1), odd)


def turn(terms, earlier, copies, token, after, rank):
    block, width = terms[0].shape
    shapes = [jax.ShapeDtypeStruct((width // rank, block * rank), jnp.float32), TOKEN]
    if earlier:
        rows = width // rank + sum(e.shape[0] for e in earlier)
        shapes.append(jax.ShapeDtypeStruct((rows, block * rank), jnp.float32))
    if copies:
        shapes.append(jax.ShapeDtypeStruct((copies, width // rank, block * rank), jnp.float32))
    return pl.pallas_call(
        functools.partial(turn_kernel, len(terms), len(earlier), copies > 0, len(after)),
        out_shape=tuple(shapes),
        in_specs=[VMEM] * (len(terms) + len(earlier) + len(after) + 1),
        out_specs=[VMEM] * len(shapes),
        scratch_shapes=[pltpu.VMEM((width // rank // UNIT, block * HALF, 2 * rank), jnp.float32)],
        compiler_params=PARAMS,
        cost_estimate=COST,
        name="turn",
    )(*after, *terms, *earlier, token)


def split(value):
    high = value.astype(jnp.bfloat16)
    return high, (value - high.astype(jnp.float32)).astype(jnp.bfloat16)


def absorb_kernel(first, start, rows_start, n_others, n_aa, n_col, n_mid, per_core, last, n_after, token, mine, *refs):
    refs = refs[n_after:]
    place = [lax.axis_index(name) for name in ("col", "ba", "aa")]
    n_rows = 0 if rows_start is None else n_col - 1
    rows_in, others_in = refs[:n_rows], refs[n_rows : n_others + n_rows]
    refs = refs[n_others + n_rows + (0 if first else 4) :]
    left, left_low, right, right_low, token_out, *outs = refs
    token_out[...] = token[...]
    count = mine.shape[0] // UNIT

    def put_left(unit, core, high, low):
        at = unit * UNIT
        row = (at // per_core) * n_col * per_core + core * per_core + at % per_core
        where = pl.ds(pl.multiple_of(row, UNIT), UNIT)
        left[where, :], left_low[where, :] = high, low

    for unit in range(count):
        high, low = split(mine[unit * UNIT : (unit + 1) * UNIT, :])
        put_left(start + unit, place[0], high, low)
        where = slice((start + unit) * UNIT, (start + unit + 1) * UNIT)
        right[0, where, :], right_low[0, where, :] = high, low
    for i, distance in enumerate(range(1, n_aa)):
        where = slice(start * UNIT, (start + count) * UNIT)
        right[distance, where, :], right_low[distance, where, :] = split(
            others_in[0][place[2] ^ distance] if n_others == 1 else others_in[i][...]
        )
    for distance in range(1, n_rows + 1):
        ref = rows_in[distance - 1]
        for unit in range(ref.shape[0] // UNIT):
            put_left(rows_start + unit, place[0] ^ distance, *split(ref[unit * UNIT : (unit + 1) * UNIT, :]))
    if not last:
        return
    scale = 1.0 / (n_mid * left.shape[1])
    share = n_mid // n_aa
    dot = functools.partial(
        lax.dot_general, dimension_numbers=(((1,), (1,)), ((), ())), preferred_element_type=jnp.float32
    )
    for distance in range(n_mid):
        goal = place[1] ^ distance
        block = (goal // share) ^ place[2]
        rows = pl.ds(pl.multiple_of((goal % share) * per_core, UNIT), per_core)
        high, low = right[block, rows, :], right_low[block, rows, :]
        both = dot(left[...], jnp.concatenate([high, low], axis=0))
        value = both[:, :per_core] + (both[:, per_core:] + dot(left_low[...], high))
        outs[distance][...] = value * scale


def absorb(token, after, mine, others, rows, held, start, rows_start, n_aa, n_col, n_mid, per_core, local_rows, last):
    depth = mine.shape[1]
    shapes = [jax.ShapeDtypeStruct((local_rows, depth), jnp.bfloat16)] * 2
    shapes += [jax.ShapeDtypeStruct((n_aa, n_mid // n_aa * per_core, depth), jnp.bfloat16)] * 2
    shapes += [TOKEN] + [jax.ShapeDtypeStruct((local_rows, per_core), jnp.float32)] * (n_mid if last else 0)
    n_in = 2 + len(after) + len(others) + len(rows)
    outs = pl.pallas_call(
        functools.partial(absorb_kernel, not held, start, rows_start, len(others), n_aa, n_col, n_mid, per_core, last, len(after)),
        out_shape=tuple(shapes),
        in_specs=[VMEM] * (n_in + len(held)),
        out_specs=[VMEM] * len(shapes),
        input_output_aliases={n_in + i: i for i in range(len(held))},
        compiler_params=PARAMS,
        cost_estimate=COST,
        name="gram" if last else "absorb",
    )(token, mine, *after, *rows, *others, *held)
    return outs[:4], outs[4], outs[5:]


def body(tensor, factor_two, factor_three):
    n_aa, n_mid, n_col = (lax.axis_size(name) for name in ("aa", "ba", "col"))
    rank = factor_three.shape[1]
    local_rows = tensor.shape[0]
    per_core = local_rows * n_aa // (n_mid * n_col)
    units = local_rows // n_col // UNIT
    bounds = [0]
    for k in range(len(CHUNKS)):
        bounds.append(round(units * sum(CHUNKS[: k + 1]) / sum(CHUNKS)))
    spans = [(a, b - a) for a, b in zip(bounds, bounds[1:]) if b > a]
    n_chunks = len(spans)
    block = rank // n_mid
    two_t, three_t = factor_two.T, factor_three.T
    token = jnp.zeros(TOKEN.shape, TOKEN.dtype)
    first_half, second_half = tuple(range(n_col // 2)), tuple(range(n_col // 2, n_col))

    sends = project(tensor, two_t, three_t, token, first_half, spans, n_mid, per_core, True)
    got = [exchange(send, "col", 1) for send in sends]
    keep = list(project(tensor, two_t, three_t, token, second_half, spans[:1], n_mid, per_core, False))
    col_steps, mid_steps = bits_of(n_col), bits_of(n_mid)
    finals, gathered = [[] for _ in spans], [None] * n_chunks
    held, mine, rows, shared, waiting, after = (), {}, {}, set(), {}, []

    def take_after():
        taken = list(after)
        after.clear()
        return taken

    def first_step(k, token):
        for step in range(1, col_steps):
            send, keep[k], token = fold(keep[k], got[k], token)
            got[k] = exchange(send, "col", 1 << step)
        (onward, final, keep[k], own), token, _ = deal(keep[k][0], got[k][0], token, take_after(), block)
        got[k] = exchange(onward, "ba", 1)
        if k == 0 and spans[1:]:
            keep.extend(project(tensor, two_t, three_t, token, second_half, spans[1:], n_mid, per_core, False))
        finals[k].append(own)
        if k in LATE:
            waiting[k] = [final]
        else:
            finals[k].append(exchange(final, "ba", 1))
        return token

    def later_steps(k, token):
        for step in range(1, mid_steps):
            (onward, final, keep[k]), token, late = deal(keep[k], got[k], token, take_after(), block, waiting.pop(k, []))
            finals[k] += [exchange(block_late, "ba", 1) for block_late in late]
            if onward is not None:
                got[k] = exchange(onward, "ba", 1 << step)
            finals[k].append(exchange(final, "ba", 1 << step))
        return token

    def finish(k, token):
        last = k == n_chunks - 1
        sent = [c for c in CORE.get(k, ()) if c < k] if k < max(CORE) else []
        sent = [c for c in range(k) if c not in shared] if last else sent
        copies = n_aa if k in WHOLE else 0
        out, token, *joined = turn(finals[k], [mine[c] for c in sent], copies, token, take_after(), rank)
        mine[k] = out
        def gather():
            if copies:
                gathered[k] = [lax.all_to_all(joined.pop(), "aa", 0, 0, tiled=True)]
            else:
                gathered[k] = [exchange(out, "aa", d) for d in range(1, n_aa)]

        source = joined[0] if sent else out
        if last or k in CORE.get(k, ()):
            shared.update(sent + [k])
            rows[k] = [exchange(source, "col", d) for d in range(1, n_col)], spans[min(sent + [k])][0]
            if k in SOON:
                after.extend(rows[k][0])
        gather()
        return token

    def take(k, token, held):
        last = k == n_chunks - 1
        others, (came, rows_start) = gathered[k], rows.get(k, ([], None))
        return absorb(
            token, take_after(), mine[k], others, came, held, spans[k][0], rows_start, n_aa, n_col, n_mid, per_core, local_rows, last
        )

    for order in ORDER:
        for name, k in order:
            if k >= n_chunks:
                continue
            if name == "first":
                token = first_step(k, token)
            elif name == "later":
                token = later_steps(k, token)
            elif name == "finish":
                token = finish(k, token)
            else:
                held, token, sums = take(k, token, held)
    gram = sums[0]
    for d in SUMS if n_mid == 4 else range(1, n_mid):
        gram = gram + exchange(sums[d], "ba", d)
    return gram


def solution(mesh):
    return jax.shard_map(
        body,
        mesh=mesh,
        in_specs=(P("aa", "ba", "col"), P("ba", None), P("col", None)),
        out_specs=P("aa", ("ba", "col")),
        check_vma=False,
    )
```
